512 devices in a mesh: row: 16 (over z, y_hi), col: 32 (over x, y_lo, core).
Axes of the slice: x: 4, y: 8 (y_hi: 2, y_lo: 4; y = y_hi * 4 + y_lo), z: 8, core: 2. Of those that a mesh axis runs over, the one named last changes fastest.
Arguments:
- fine_queries: bfloat16 [16, 32, 128, 512], P('row', 'col'), may hold values from -288 to 288
- fine_keys: bfloat16 [16, 32, 128, 512], P('row', 'col'), may hold values from -6 to 6
- fine_values: bfloat16 [16, 32, 128, 512], P('row', 'col'), may hold values from -6 to 6
- grad_out: bfloat16 [16, 32, 128, 512], P('row', 'col'), may hold values from -6 to 6
- coarse_keys: bfloat16 [512, 512], P(('row', 'col')), may hold values from -6 to 6
- coarse_values: bfloat16 [512, 512], P(('row', 'col')), may hold values from -6 to 6
- tile_counts: int32 [16, 32], replicated, may hold values from 1 to 128, as said below
Outputs:
- grad_q: bfloat16 [16, 32, 128, 512], P('row', 'col')
- grad_k: bfloat16 [16, 32, 128, 512], P('row', 'col')
- grad_v: bfloat16 [16, 32, 128, 512], P('row', 'col')
- grad_coarse_k: float32 [512, 512], P(('row', 'col'))
- grad_coarse_v: float32 [512, 512], P(('row', 'col'))
The draws below stay inside these ranges and needn't reach their ends.
Inputs may be any that keep to these rules, and one draw needn't show every extreme that they name: `tile_counts`: live fine tokens of each tile; some tile has all 128 slots live.
All inputs are finite; a program needn't handle non-finite values.
Results may differ from the reference program's by a relative error of at most 0.0075.
Values may be sent and summed in bfloat16 or wider, within the bound.
No kernel may reach another device: no remote copies, remote signals or barrier semaphores. Data moves between devices by JAX's collectives and lax.ppermute only.
A program may use at most 64 MiB of HBM per device.

```python
import jax
import jax.numpy as jnp
from jax import lax

HEADS = 8
HEAD_DIM = 64
D = 512
FINE_DEV = 128
COARSE = 512
N_ROW = 16
N_COL = 32


def shared_keys(key):
    shape = (N_ROW, N_COL, FINE_DEV, HEADS * HEAD_DIM)
    return jnp.clip(jax.random.normal(key, shape, jnp.float32), -6.0, 6.0)


def draw_fine_keys(key, part):
    common = shared_keys(key)
    return common.astype(jnp.bfloat16)


def draw_fine_queries(key, part):
    common = shared_keys(key)
    key = jax.random.fold_in(key, 2)
    fresh = jnp.clip(jax.random.normal(key, common.shape, jnp.float32), -6.0, 6.0)
    return fresh.astype(jnp.bfloat16)


def draw_tile_counts(key, part):
    key = jax.random.fold_in(key, 3)
    tiles = N_ROW * N_COL
    picks = jax.random.randint(jax.random.fold_in(key, 1), (tiles,), 0, 4)
    levels = jnp.maximum(picks - 1, 0)
    full = FINE_DEV // jnp.power(4, levels)
    jitter = jax.random.randint(jax.random.fold_in(key, 2), (tiles,), 0, 1 << 30) % (full // 4 + 1)
    counts = jnp.maximum(full - jitter, 1)
    chosen = jax.random.randint(jax.random.fold_in(key, 4), (), 0, tiles)
    counts = jnp.where(jnp.arange(tiles) == chosen, FINE_DEV, counts)
    return counts.reshape(N_ROW, N_COL).astype(jnp.int32)


def shard_levels(key, extent, split, smallest, top_value):
    gain, own = 1.0, jax.random.fold_in(key, 6)
    for dim, blocks in split:
        steps = jnp.exp(jax.random.uniform(jax.random.fold_in(own, dim), (blocks,), jnp.float32, smallest / len(split), top_value / len(split)))
        gain = gain * jnp.repeat(steps, extent[dim] // blocks).reshape([-1 if axis == dim else 1 for axis in range(len(extent))])
    return gain


def normal_values(key, shape, deviation, bound, cuts=(), held_as=jnp.bfloat16):
    factor_of = shard_levels(key, shape, cuts, -0.22, 0.18) if cuts else 1.0
    drawn = jax.random.normal(key, shape, jnp.float32) * deviation * factor_of
    return jnp.minimum(jnp.maximum(drawn, -bound), bound).astype(held_as)


def setup_inputs(seed: int = 0) -> dict:
    seeds = jax.random.split(jax.random.key(seed), 8)
    fine_queries = draw_fine_queries(jax.random.fold_in(seeds[7], 71), 0)
    fine_keys = draw_fine_keys(jax.random.fold_in(seeds[7], 71), 0)
    fine_values = normal_values(seeds[2], (N_ROW, N_COL, FINE_DEV, D), 1.0, 6.0, ((0, 16), (1, 32)))
    grad_out = normal_values(seeds[3], (N_ROW, N_COL, FINE_DEV, D), 1.0, 6.0, ((0, 16), (1, 32)))
    coarse_keys = normal_values(seeds[4], (COARSE, D), 1.0, 6.0, ((0, 512),))
    coarse_values = normal_values(seeds[5], (COARSE, D), 1.0, 6.0, ((0, 512),))
    tile_counts = draw_tile_counts(jax.random.fold_in(seeds[7], 71), 0)
    return dict(fine_queries=fine_queries, fine_keys=fine_keys, fine_values=fine_values, grad_out=grad_out, coarse_keys=coarse_keys, coarse_values=coarse_values, tile_counts=tile_counts)


def split_heads(matrix):
    return matrix.astype(jnp.float32).reshape(matrix.shape[0], HEADS, HEAD_DIM)


def reference(fine_queries, fine_keys, fine_values, grad_out, coarse_keys, coarse_values, tile_counts):
    width = HEADS * HEAD_DIM
    scale = HEAD_DIM ** -0.5
    edges = ((1, 1), (1, 1), (0, 0), (0, 0))
    padded_keys = jnp.pad(fine_keys, edges)
    padded_values = jnp.pad(fine_values, edges)
    padded_counts = jnp.pad(tile_counts, 1)
    coarse_heads_k = split_heads(coarse_keys)
    coarse_heads_v = split_heads(coarse_values)
    positions = jnp.arange(FINE_DEV, dtype=jnp.int32)
    coarse_live = jnp.ones((COARSE,), dtype=bool)
    zero = jnp.int32(0)
    fine_count = 9 * FINE_DEV

    def add_block(total, terms, row_at, col_at):
        block = terms[:fine_count].reshape(3, 3, FINE_DEV, width)
        start = (row_at, col_at, zero, zero)
        return lax.dynamic_update_slice(total, lax.dynamic_slice(total, start, block.shape) + block, start)

    def visit(carry, tile):
        key_total, value_total, coarse_key_total, coarse_value_total = carry
        row_at = (tile // N_COL).astype(jnp.int32)
        col_at = (tile % N_COL).astype(jnp.int32)
        near_keys = lax.dynamic_slice(padded_keys, (row_at, col_at, zero, zero), (3, 3, FINE_DEV, width)).reshape(fine_count, width)
        near_values = lax.dynamic_slice(padded_values, (row_at, col_at, zero, zero), (3, 3, FINE_DEV, width)).reshape(fine_count, width)
        near_counts = lax.dynamic_slice(padded_counts, (row_at, col_at), (3, 3)).reshape(9)
        key_live = jnp.concatenate([(positions[None, :] < near_counts[:, None]).reshape(-1), coarse_live])
        query_live = positions < tile_counts[row_at, col_at]
        keys = jnp.concatenate([split_heads(near_keys), coarse_heads_k], axis=0)
        values = jnp.concatenate([split_heads(near_values), coarse_heads_v], axis=0)
        query = split_heads(lax.dynamic_slice(fine_queries, (row_at, col_at, zero, zero), (1, 1, FINE_DEV, width))[0, 0])
        upstream = split_heads(lax.dynamic_slice(grad_out, (row_at, col_at, zero, zero), (1, 1, FINE_DEV, width))[0, 0])
        scores = jnp.einsum('qhd,khd->hqk', query, keys) * scale
        masked = jnp.where(key_live[None, None, :], scores, -1e30)
        peak = jnp.max(masked, axis=-1, keepdims=True)
        lse = peak + jnp.log(jnp.sum(jnp.exp(masked - peak), axis=-1, keepdims=True))
        valid = query_live[None, :, None] & key_live[None, None, :]
        probs = jnp.where(valid, jnp.exp(scores - lse), 0.0)
        probs_low = lax.optimization_barrier(probs.astype(jnp.bfloat16)).astype(jnp.float32)
        attended = jnp.einsum('hqk,khd->qhd', probs_low, values)
        delta = jnp.sum(upstream * attended, axis=-1)
        grad_probs = jnp.einsum('qhd,khd->hqk', upstream, values)
        grad_scores = probs * (grad_probs - delta.T[:, :, None])
        grad_low = lax.optimization_barrier(grad_scores.astype(jnp.bfloat16)).astype(jnp.float32)
        grad_query = (jnp.einsum('hqk,khd->qhd', grad_low, keys) * scale).reshape(FINE_DEV, width).astype(jnp.bfloat16)
        key_terms = jnp.einsum('hqk,qhd->khd', grad_low, query).reshape(-1, width) * scale
        value_terms = jnp.einsum('hqk,qhd->khd', probs_low, upstream).reshape(-1, width)
        key_total = add_block(key_total, key_terms, row_at, col_at)
        value_total = add_block(value_total, value_terms, row_at, col_at)
        coarse_key_total = coarse_key_total + key_terms[fine_count:]
        coarse_value_total = coarse_value_total + value_terms[fine_count:]
        return (key_total, value_total, coarse_key_total, coarse_value_total), grad_query

    grid_zeros = jnp.zeros((N_ROW + 2, N_COL + 2, FINE_DEV, width), jnp.float32)
    coarse_zeros = jnp.zeros((COARSE, width), jnp.float32)
    carry, grad_rows = lax.scan(visit, (grid_zeros, grid_zeros, coarse_zeros, coarse_zeros), jnp.arange(N_ROW * N_COL, dtype=jnp.int32))
    key_total, value_total, coarse_key_total, coarse_value_total = carry
    grad_q = grad_rows.reshape(N_ROW, N_COL, FINE_DEV, width)
    grad_k = key_total[1:-1, 1:-1].astype(jnp.bfloat16)
    grad_v = value_total[1:-1, 1:-1].astype(jnp.bfloat16)
    return (grad_q, grad_k, grad_v, coarse_key_total, coarse_value_total)
```

```python
import functools

import jax
import jax.numpy as jnp
from jax import lax
from jax.experimental import pallas as pl
from jax.experimental.pallas import tpu as pltpu
from jax.sharding import PartitionSpec as P

HEAD_DIM = 64
LANES = 128
SCALE = HEAD_DIM ** (-0.5)
NEGATIVE = -1e30

GATHER_ORDER = (
    ("row", 8),
    ("row", 4),
    ("col", 16),
    ("row", 1),
    ("col", 4),
    ("row", 2),
    ("col", 8),
    ("col", 2),
    ("col", 1),
)


def exchange(block, axis, bit):
    return lax.ppermute(block, axis, [(i, i ^ bit) for i in range(lax.axis_size(axis))])


def to_far(block, axis):
    size = lax.axis_size(axis)
    return lax.ppermute(block, axis, [(i, (i + (1 if i % 2 else -1)) % size) for i in range(size)])


def skip_row(block, way):
    size = lax.axis_size("row")
    return lax.ppermute(block, "row", [(i, (i + (-way if i % 2 else way)) % size) for i in range(size)])


def gather_steps():
    return [(axis, bit) for axis, bit in GATHER_ORDER if bit < lax.axis_size(axis)]


def gather_coarse(own):
    width = own.shape[-1]
    block = own.reshape(1, 8, width // 8)
    for axis, bit in gather_steps():
        block = jnp.concatenate([block, exchange(block, axis, bit)], axis=0)
        if block.ndim == 3 and block.shape[0] == 16:
            block = block.reshape(16, width)
    return block


def scatter_coarse(lower, upper):
    steps = gather_steps()[::-1]
    for number, (axis, bit) in enumerate(steps):
        lower = lower + exchange(upper, axis, bit).astype(jnp.float32)
        if number + 1 < len(steps):
            half = lower.shape[0] // 2
            lower, upper = lower[:half], lower[half:]
            if half >= 64:
                upper = upper.astype(jnp.bfloat16)
    return lower


def attention_kernel(
    counts, q_ref, g_ref, own_ref, near_ref, far_ref, coarse_ref,
    dq_ref, own_out, near_out, far_out, low_out, high_out, p_ref, dp_ref,
):
    rows, width = q_ref.shape
    coarse_count = coarse_ref.shape[0]
    half = coarse_count // 2
    step = min(rows, half)
    tiles = []
    for column, (ref, out) in enumerate(((own_ref, own_out), (near_ref, near_out), (far_ref, far_out))):
        for line in range(3):
            tiles.append((ref.at[line], out.at[line], 0, rows, counts[column * 3 + line]))
    for start in range(0, coarse_count, step):
        out = (low_out, start) if start < half else (high_out, start - half)
        tiles.append((coarse_ref.at[start : start + step], out[0].at[out[1] : out[1] + step], 0, step, None))
    starts = []
    total = 0
    for tile in tiles:
        starts.append(total)
        total += tile[3]
    contract_last = (((1,), (1,)), ((), ()))
    contract_first = (((0,), (0,)), ((), ()))
    f32 = jnp.float32

    def stacked(block):
        first = lax.broadcasted_iota(jnp.int32, block.shape, 1) < HEAD_DIM
        zero = jnp.zeros_like(block)
        return jnp.concatenate([jnp.where(first, block, zero), jnp.where(first, zero, block)], axis=0)

    query_at = lax.broadcasted_iota(jnp.int32, (1, 2 * rows), 1)
    query_at = jnp.where(query_at >= rows, query_at - rows, query_at)
    query_live = (query_at < counts[9]).astype(f32)

    def pair(number, carry):
        lane = pl.multiple_of(number * LANES, LANES)
        at_k = pl.ds(lane, LANES)
        at_v = pl.ds(pl.multiple_of(width + number * LANES, LANES), LANES)
        query = stacked(q_ref[:, at_k] * jnp.asarray(SCALE, q_ref.dtype))
        upstream = stacked(g_ref[:, at_k])
        peak = jnp.full((1, 2 * rows), NEGATIVE, f32)
        for (ref, _, _, size, count), start in zip(tiles, starts):
            scores = lax.dot_general(ref[:, at_k], query, contract_last, preferred_element_type=f32)
            if count is not None:
                live = lax.broadcasted_iota(jnp.int32, scores.shape, 0) < count
                scores = jnp.where(live, scores, NEGATIVE)
            p_ref[start : start + size, :] = scores
            peak = jnp.maximum(peak, jnp.max(scores, axis=0, keepdims=True))
        norm = jnp.zeros((1, 2 * rows), f32)
        for (_, _, _, size, _), start in zip(tiles, starts):
            weights = jnp.exp(p_ref[start : start + size, :] - peak)
            p_ref[start : start + size, :] = weights
            norm = norm + jnp.sum(weights, axis=0, keepdims=True)
        inverse = query_live / norm
        delta = jnp.zeros((1, 2 * rows), f32)
        for (ref, out, _, size, _), start in zip(tiles, starts):
            probs = p_ref[start : start + size, :] * inverse
            probs_low = probs.astype(jnp.bfloat16)
            p_ref[start : start + size, :] = probs
            grad_probs = lax.dot_general(ref[:, at_v], upstream, contract_last, preferred_element_type=f32)
            dp_ref[start : start + size, :] = grad_probs
            delta = delta + jnp.sum(probs_low.astype(f32) * grad_probs, axis=0, keepdims=True)
            value_terms = jnp.dot(probs_low, upstream, preferred_element_type=f32)
            out[:, at_v] = value_terms.astype(out.dtype)
        grad_query = jnp.zeros((LANES, 2 * rows), f32)
        for (ref, out, _, size, _), start in zip(tiles, starts):
            span = slice(start, start + size)
            grad_low = (p_ref[span, :] * (dp_ref[span, :] - delta)).astype(jnp.bfloat16)
            key_terms = jnp.dot(grad_low, query, preferred_element_type=f32)
            out[:, at_k] = key_terms.astype(out.dtype)
            grad_query = grad_query + lax.dot_general(
                ref[:, at_k], grad_low, contract_first, preferred_element_type=f32
            )
        both = jnp.concatenate([grad_query[:HEAD_DIM, :rows], grad_query[HEAD_DIM:, rows:]], axis=0)
        dq_ref[:, at_k] = (both.T * SCALE).astype(dq_ref.dtype)
        return carry

    lax.fori_loop(0, width // LANES, pair, 0)


def attention(counts, query, upstream, own, near, far, coarse):
    rows, width = query.shape
    double = 2 * width
    coarse_count = coarse.shape[0]
    keys = 9 * rows + coarse_count
    in_vmem = pl.BlockSpec(memory_space=pltpu.VMEM)
    work = 2 * rows * keys * width
    return pl.pallas_call(
        attention_kernel,
        out_shape=(
            jax.ShapeDtypeStruct((rows, width), jnp.bfloat16),
            jax.ShapeDtypeStruct((3, rows, double), jnp.float32),
            jax.ShapeDtypeStruct((3, rows, double), jnp.bfloat16),
            jax.ShapeDtypeStruct((3, rows, double), jnp.bfloat16),
            jax.ShapeDtypeStruct((coarse_count // 2, double), jnp.float32),
            jax.ShapeDtypeStruct((coarse_count // 2, double), jnp.bfloat16),
        ),
        in_specs=[pl.BlockSpec(memory_space=pltpu.SMEM)] + [in_vmem] * 6,
        out_specs=(in_vmem,) * 6,
        scratch_shapes=[
            pltpu.VMEM((keys, 2 * rows), jnp.float32),
            pltpu.VMEM((keys, 2 * rows), jnp.float32),
        ],
        compiler_params=pltpu.CompilerParams(vmem_limit_bytes=40 * 2**20),
        cost_estimate=pl.CostEstimate(
            flops=5 * work, bytes_accessed=12 * 2**20, transcendentals=rows * keys * width // HEAD_DIM
        ),
    )(counts, query, upstream, own, near, far, coarse)


def neighbour_counts(tile_counts):
    places = []
    for axis, size in zip(("row", "col"), tile_counts.shape):
        here = lax.axis_index(axis)
        odd = here % 2
        near = here + 1 - 2 * odd
        far = here - 1 + 2 * odd
        at = jnp.stack([here, near, far])
        places.append((at.clip(0, size - 1), (at >= 0) & (at < size)))
    (row_at, row_in), (col_at, col_in) = places
    found = tile_counts[row_at[None, :], col_at[:, None]]
    found = jnp.where(row_in[None, :] & col_in[:, None], found, 0).reshape(9)
    return jnp.concatenate([found, found[:1]]).astype(jnp.int32)


def per_device(
    fine_queries, fine_keys, fine_values, grad_out, coarse_keys, coarse_values, tile_counts
):
    rows, width = fine_queries.shape[2:]
    counts = neighbour_counts(tile_counts)
    fine = jnp.concatenate([fine_keys[0, 0], fine_values[0, 0]], axis=-1)
    paired = exchange(fine, "row", 1)
    coarse = gather_coarse(jnp.concatenate([coarse_keys, coarse_values], axis=-1))
    far = skip_row(paired, 2)
    own_column = jnp.stack([fine, paired, far])
    near_column = exchange(own_column, "col", 1)
    far_column = to_far(own_column, "col")
    grad_q, own_terms, near_terms, far_terms, coarse_low, coarse_high = attention(
        counts, fine_queries[0, 0], grad_out[0, 0], own_column, near_column, far_column, coarse
    )
    coarse_sum = scatter_coarse(coarse_low, coarse_high)
    line = (
        own_terms
        + exchange(near_terms, "col", 1).astype(jnp.float32)
        + to_far(far_terms, "col").astype(jnp.float32)
    )
    low = jnp.bfloat16
    forwarded = skip_row(line[2].astype(low), -2).astype(jnp.float32)
    returned = exchange((line[1] + forwarded).astype(low), "row", 1).astype(jnp.float32)
    total = (line[0] + returned).astype(low)
    return (
        grad_q[None, None],
        total[None, None, :, :width],
        total[None, None, :, width:],
        coarse_sum[:, :width],
        coarse_sum[:, width:],
    )


def solution(mesh):
    return jax.shard_map(
        per_device,
        mesh=mesh,
        in_specs=(
            P("row", "col", None, None),
            P("row", "col", None, None),
            P("row", "col", None, None),
            P("row", "col", None, None),
            P(("row", "col"), None),
            P(("row", "col"), None),
            P(),
        ),
        out_specs=(
            P("row", "col", None, None),
            P("row", "col", None, None),
            P("row", "col", None, None),
            P(("row", "col"), None),
            P(("row", "col"), None),
        ),
        check_vma=False,
    )
```

```python
import jax
import jax.numpy as jnp
from jax import lax
from jax.experimental import pallas as pl
from jax.experimental.pallas import tpu as pltpu
from jax.sharding import PartitionSpec as P

HEAD_DIM = 64
LANES = 128
SCALE = HEAD_DIM ** (-0.5)
NEGATIVE = -1e30

def exchange(block, axis, bit):
    return lax.ppermute(block, axis, [(i, i ^ bit) for i in range(lax.axis_size(axis))])


def to_far(block, axis):
    size = lax.axis_size(axis)
    return lax.ppermute(block, axis, [(i, (i + (1 if i % 2 else -1)) % size) for i in range(size)])


def skip_row(block, way):
    size = lax.axis_size("row")
    return lax.ppermute(block, "row", [(i, (i + (-way if i % 2 else way)) % size) for i in range(size)])


def same_core():
    size = lax.axis_size("col")
    return [list(range(core, size, 2)) for core in range(2)]


def deal(block, axis, groups=None):
    return lax.all_to_all(block, axis, 0, 0, axis_index_groups=groups, tiled=True)


def gather_coarse(own):
    width = own.shape[-1]
    lines = lax.axis_size("row")
    members = lax.axis_size("col") // 2
    block = jnp.broadcast_to(own.reshape(1, 8, width // 8), (lines, 8, width // 8))
    block = deal(block, "row").reshape(1, lines, width)
    block = deal(jnp.broadcast_to(block, (members, lines, width)), "col", same_core())
    return block.reshape(members * lines, width)


def scatter_coarse(kept, other):
    width = kept.shape[-1]
    lines = lax.axis_size("row")
    members = lax.axis_size("col") // 2
    block = (kept + exchange(other, "col", 1).astype(jnp.float32)).astype(jnp.bfloat16)
    block = deal(block.reshape(members, lines, width), "col", same_core()).astype(jnp.float32).sum(axis=0)
    block = deal(block.reshape(lines, 8, width // 8), "row").sum(axis=0)
    return block.reshape(1, width)


def attention_kernel(
    counts, q_ref, g_ref, own_ref, near_ref, far_ref, kept_ref, other_ref,
    dq_ref, own_out, near_out, far_out, kept_out, other_out, p_ref, dp_ref,
):
    rows, width = q_ref.shape
    coarse_count = kept_ref.shape[0]
    step = min(rows, coarse_count)
    tiles = []
    for column, (ref, out) in enumerate(((own_ref, own_out), (near_ref, near_out), (far_ref, far_out))):
        for line in range(3):
            tiles.append((ref.at[line], out.at[line], rows, counts[column * 3 + line]))
    for ref, out in ((kept_ref, kept_out), (other_ref, other_out)):
        for start in range(0, coarse_count, step):
            span = slice(start, start + step)
            tiles.append((ref.at[span], out.at[span], step, None))
    starts = []
    total = 0
    for tile in tiles:
        starts.append(total)
        total += tile[2]
    contract_last = (((1,), (1,)), ((), ()))
    contract_first = (((0,), (0,)), ((), ()))
    f32 = jnp.float32

    def stacked(block):
        first = lax.broadcasted_iota(jnp.int32, block.shape, 1) < HEAD_DIM
        zero = jnp.zeros_like(block)
        return jnp.concatenate([jnp.where(first, block, zero), jnp.where(first, zero, block)], axis=0)

    query_at = lax.broadcasted_iota(jnp.int32, (1, 2 * rows), 1)
    query_at = jnp.where(query_at >= rows, query_at - rows, query_at)
    query_live = (query_at < counts[9]).astype(f32)

    def pair(number, carry):
        lane = pl.multiple_of(number * LANES, LANES)
        at_k = pl.ds(lane, LANES)
        at_v = pl.ds(pl.multiple_of(width + number * LANES, LANES), LANES)
        query = stacked(q_ref[:, at_k] * jnp.asarray(SCALE, q_ref.dtype))
        upstream = stacked(g_ref[:, at_k])
        peak = jnp.full((1, 2 * rows), NEGATIVE, f32)
        for (ref, _, size, count), start in zip(tiles, starts):
            scores = lax.dot_general(ref[:, at_k], query, contract_last, preferred_element_type=f32)
            if count is not None:
                live = lax.broadcasted_iota(jnp.int32, scores.shape, 0) < count
                scores = jnp.where(live, scores, NEGATIVE)
            p_ref[start : start + size, :] = scores
            peak = jnp.maximum(peak, jnp.max(scores, axis=0, keepdims=True))
        norm = jnp.zeros((1, 2 * rows), f32)
        for (_, _, size, _), start in zip(tiles, starts):
            weights = jnp.exp(p_ref[start : start + size, :] - peak)
            p_ref[start : start + size, :] = weights
            norm = norm + jnp.sum(weights, axis=0, keepdims=True)
        inverse = query_live / norm
        delta = jnp.zeros((1, 2 * rows), f32)
        for (ref, out, size, _), start in zip(tiles, starts):
            probs = p_ref[start : start + size, :] * inverse
            probs_low = probs.astype(jnp.bfloat16)
            p_ref[start : start + size, :] = probs
            grad_probs = lax.dot_general(ref[:, at_v], upstream, contract_last, preferred_element_type=f32)
            dp_ref[start : start + size, :] = grad_probs
            delta = delta + jnp.sum(probs_low.astype(f32) * grad_probs, axis=0, keepdims=True)
            value_terms = jnp.dot(probs_low, upstream, preferred_element_type=f32)
            out[:, at_v] = value_terms.astype(out.dtype)
        grad_query = jnp.zeros((LANES, 2 * rows), f32)
        for (ref, out, size, _), start in zip(tiles, starts):
            span = slice(start, start + size)
            grad_low = (p_ref[span, :] * (dp_ref[span, :] - delta)).astype(jnp.bfloat16)
            key_terms = jnp.dot(grad_low, query, preferred_element_type=f32)
            out[:, at_k] = key_terms.astype(out.dtype)
            grad_query = grad_query + lax.dot_general(
                ref[:, at_k], grad_low, contract_first, preferred_element_type=f32
            )
        both = jnp.concatenate([grad_query[:HEAD_DIM, :rows], grad_query[HEAD_DIM:, rows:]], axis=0)
        dq_ref[:, at_k] = (both.T * SCALE).astype(dq_ref.dtype)
        return carry

    lax.fori_loop(0, width // LANES, pair, 0)


def attention(counts, query, upstream, own, near, far, kept, other):
    rows, width = query.shape
    double = 2 * width
    coarse_count = kept.shape[0]
    keys = 9 * rows + 2 * coarse_count
    in_vmem = pl.BlockSpec(memory_space=pltpu.VMEM)
    work = 2 * rows * keys * width
    return pl.pallas_call(
        attention_kernel,
        out_shape=(
            jax.ShapeDtypeStruct((rows, width), jnp.bfloat16),
            jax.ShapeDtypeStruct((3, rows, double), jnp.float32),
            jax.ShapeDtypeStruct((3, rows, double), jnp.bfloat16),
            jax.ShapeDtypeStruct((3, rows, double), jnp.bfloat16),
            jax.ShapeDtypeStruct((coarse_count, double), jnp.float32),
            jax.ShapeDtypeStruct((coarse_count, double), jnp.bfloat16),
        ),
        in_specs=[pl.BlockSpec(memory_space=pltpu.SMEM)] + [in_vmem] * 7,
        out_specs=(in_vmem,) * 6,
        scratch_shapes=[
            pltpu.VMEM((keys, 2 * rows), jnp.float32),
            pltpu.VMEM((keys, 2 * rows), jnp.float32),
        ],
        compiler_params=pltpu.CompilerParams(vmem_limit_bytes=40 * 2**20),
        cost_estimate=pl.CostEstimate(
            flops=5 * work, bytes_accessed=12 * 2**20, transcendentals=rows * keys * width // HEAD_DIM
        ),
    )(counts, query, upstream, own, near, far, kept, other)


def neighbour_counts(tile_counts):
    places = []
    for axis, size in zip(("row", "col"), tile_counts.shape):
        here = lax.axis_index(axis)
        odd = here % 2
        near = here + 1 - 2 * odd
        far = here - 1 + 2 * odd
        at = jnp.stack([here, near, far])
        places.append((at.clip(0, size - 1), (at >= 0) & (at < size)))
    (row_at, row_in), (col_at, col_in) = places
    found = tile_counts[row_at[None, :], col_at[:, None]]
    found = jnp.where(row_in[None, :] & col_in[:, None], found, 0).reshape(9)
    return jnp.concatenate([found, found[:1]]).astype(jnp.int32)


def per_device(
    fine_queries, fine_keys, fine_values, grad_out, coarse_keys, coarse_values, tile_counts
):
    rows, width = fine_queries.shape[2:]
    counts = neighbour_counts(tile_counts)
    fine = jnp.concatenate([fine_keys[0, 0], fine_values[0, 0]], axis=-1)
    paired = exchange(fine, "row", 1)
    kept = gather_coarse(jnp.concatenate([coarse_keys, coarse_values], axis=-1))
    far = skip_row(paired, 2)
    own_column = jnp.stack([fine, paired, far])
    near_column = exchange(own_column, "col", 1)
    far_column = to_far(own_column, "col")
    other = exchange(kept, "col", 1)
    grad_q, own_terms, near_terms, far_terms, kept_terms, other_terms = attention(
        counts, fine_queries[0, 0], grad_out[0, 0], own_column, near_column, far_column, kept, other
    )
    coarse_sum = scatter_coarse(kept_terms, other_terms)
    line = (
        own_terms
        + exchange(near_terms, "col", 1).astype(jnp.float32)
        + to_far(far_terms, "col").astype(jnp.float32)
    )
    low = jnp.bfloat16
    forwarded = skip_row(line[2].astype(low), -2).astype(jnp.float32)
    returned = exchange((line[1] + forwarded).astype(low), "row", 1).astype(jnp.float32)
    total = (line[0] + returned).astype(low)
    return (
        grad_q[None, None],
        total[None, None, :, :width],
        total[None, None, :, width:],
        coarse_sum[:, :width],
        coarse_sum[:, width:],
    )


def solution(mesh):
    return jax.shard_map(
        per_device,
        mesh=mesh,
        in_specs=(
            P("row", "col", None, None),
            P("row", "col", None, None),
            P("row", "col", None, None),
            P("row", "col", None, None),
            P(("row", "col"), None),
            P(("row", "col"), None),
            P(),
        ),
        out_specs=(
            P("row", "col", None, None),
            P("row", "col", None, None),
            P("row", "col", None, None),
            P(("row", "col"), None),
            P(("row", "col"), None),
        ),
        check_vma=False,
    )
```

```python
import jax
import jax.numpy as jnp
from jax import lax
from jax.experimental import pallas as pl
from jax.experimental.pallas import tpu as pltpu
from jax.sharding import PartitionSpec as P

HEAD_DIM = 64
LANES = 128
SCALE = HEAD_DIM ** (-0.5)
NEGATIVE = -1e30

def exchange(block, axis, bit):
    return lax.ppermute(block, axis, [(i, i ^ bit) for i in range(lax.axis_size(axis))])


def to_far(block, axis):
    size = lax.axis_size(axis)
    return lax.ppermute(block, axis, [(i, (i + (1 if i % 2 else -1)) % size) for i in range(size)])


def skip_row(block, way):
    size = lax.axis_size("row")
    return lax.ppermute(block, "row", [(i, (i + (-way if i % 2 else way)) % size) for i in range(size)])


def place_groups():
    lines, columns = lax.axis_size("row"), lax.axis_size("col")
    half = columns // 2
    first = [
        [(z + y_hi) * columns + x_hi + x_lo + y_lo + core for x_hi in (0, half) for y_hi in range(2) for y_lo in range(0, 8, 2)]
        for z in range(0, lines, 2)
        for x_lo in range(0, half, 8)
        for core in range(2)
    ]
    second = [
        [(z + y_hi) * columns + x_hi + x_lo + y_lo + core for x_lo in range(0, half, 8) for z in range(0, lines, 2)]
        for x_hi in (0, half)
        for y_hi in range(2)
        for y_lo in range(0, 8, 2)
        for core in range(2)
    ]
    return first, second


def deal(block, groups):
    return lax.all_to_all(block, ("row", "col"), 0, 0, axis_index_groups=groups, tiled=True)


def gather_first(own):
    width = own.shape[-1]
    groups, _ = place_groups()
    members = len(groups[0])
    block = jnp.broadcast_to(own.reshape(1, 8, width // 8), (members, 8, width // 8))
    return deal(block, groups).reshape(members, width)


def gather_second(block):
    held, width = block.shape
    _, groups = place_groups()
    members = len(groups[0])
    return deal(jnp.broadcast_to(block, (members, held, width)), groups).reshape(members * held, width)


def scatter_coarse(block):
    width = block.shape[-1]
    first, second = place_groups()
    held = len(first[0])
    block = deal(block.reshape(len(second[0]), held, width), second).astype(jnp.float32).sum(axis=0)
    block = deal(block.reshape(held, 8, width // 8), first).sum(axis=0)
    return block.reshape(1, width)


def attention_kernel(
    counts, q_ref, g_ref, own_ref, pair_ref, skip_ref, near_own_ref, near_ref, far_own_ref, far_ref, kept_ref, other_ref,
    dq_ref, own_out, core_out, far_own_out, far_out, kept_out, p_ref, dp_ref,
):
    rows, width = q_ref.shape
    coarse_count = kept_ref.shape[0]
    step = min(rows, coarse_count)
    fine_in = (own_ref, pair_ref, skip_ref, near_own_ref, near_ref.at[0], near_ref.at[1], far_own_ref, far_ref.at[0], far_ref.at[1])
    fine_out = [own_out.at[at] for at in range(3)]
    fine_out += [core_out.at[at * rows : (at + 1) * rows] for at in range(3)]
    fine_out += [far_own_out, far_out.at[0], far_out.at[1]]
    tiles = [(fine_in[at], fine_out[at], rows, counts[at]) for at in range(9)]
    for ref, out, ahead in ((kept_ref, kept_out, 0), (other_ref, core_out, 3 * rows)):
        for start in range(0, coarse_count, step):
            tiles.append((ref.at[start : start + step], out.at[ahead + start : ahead + start + step], step, None))
    starts = []
    total = 0
    for tile in tiles:
        starts.append(total)
        total += tile[2]
    contract_last = (((1,), (1,)), ((), ()))
    contract_first = (((0,), (0,)), ((), ()))
    f32 = jnp.float32

    def stacked(block):
        first = lax.broadcasted_iota(jnp.int32, block.shape, 1) < HEAD_DIM
        zero = jnp.zeros_like(block)
        return jnp.concatenate([jnp.where(first, block, zero), jnp.where(first, zero, block)], axis=0)

    query_at = lax.broadcasted_iota(jnp.int32, (1, 2 * rows), 1)
    query_at = jnp.where(query_at >= rows, query_at - rows, query_at)
    query_live = (query_at < counts[9]).astype(f32)

    def pair(number, carry):
        lane = pl.multiple_of(number * LANES, LANES)
        at_k = pl.ds(lane, LANES)
        at_v = pl.ds(pl.multiple_of(width + number * LANES, LANES), LANES)
        query = stacked(q_ref[:, at_k] * jnp.asarray(SCALE, q_ref.dtype))
        upstream = stacked(g_ref[:, at_k])
        peak = jnp.full((1, 2 * rows), NEGATIVE, f32)
        for (ref, _, size, count), start in zip(tiles, starts):
            scores = lax.dot_general(ref[:, at_k], query, contract_last, preferred_element_type=f32)
            if count is not None:
                live = lax.broadcasted_iota(jnp.int32, scores.shape, 0) < count
                scores = jnp.where(live, scores, NEGATIVE)
            p_ref[start : start + size, :] = scores
            peak = jnp.maximum(peak, jnp.max(scores, axis=0, keepdims=True))
        norm = jnp.zeros((1, 2 * rows), f32)
        for (_, _, size, _), start in zip(tiles, starts):
            weights = jnp.exp(p_ref[start : start + size, :] - peak)
            p_ref[start : start + size, :] = weights
            norm = norm + jnp.sum(weights, axis=0, keepdims=True)
        inverse = query_live / norm
        delta = jnp.zeros((1, 2 * rows), f32)
        for (ref, out, size, _), start in zip(tiles, starts):
            probs = p_ref[start : start + size, :] * inverse
            probs_low = probs.astype(jnp.bfloat16)
            p_ref[start : start + size, :] = probs
            grad_probs = lax.dot_general(ref[:, at_v], upstream, contract_last, preferred_element_type=f32)
            dp_ref[start : start + size, :] = grad_probs
            delta = delta + jnp.sum(probs_low.astype(f32) * grad_probs, axis=0, keepdims=True)
            value_terms = jnp.dot(probs_low, upstream, preferred_element_type=f32)
            out[:, at_v] = value_terms.astype(out.dtype)
        grad_query = jnp.zeros((LANES, 2 * rows), f32)
        for (ref, out, size, _), start in zip(tiles, starts):
            span = slice(start, start + size)
            grad_low = (p_ref[span, :] * (dp_ref[span, :] - delta)).astype(jnp.bfloat16)
            key_terms = jnp.dot(grad_low, query, preferred_element_type=f32)
            out[:, at_k] = key_terms.astype(out.dtype)
            grad_query = grad_query + lax.dot_general(
                ref[:, at_k], grad_low, contract_first, preferred_element_type=f32
            )
        both = jnp.concatenate([grad_query[:HEAD_DIM, :rows], grad_query[HEAD_DIM:, rows:]], axis=0)
        dq_ref[:, at_k] = (both.T * SCALE).astype(dq_ref.dtype)
        return carry

    lax.fori_loop(0, width // LANES, pair, 0)


def attention(counts, query, upstream, *blocks):
    rows, width = query.shape
    double = 2 * width
    coarse_count = blocks[-1].shape[0]
    keys = 9 * rows + 2 * coarse_count
    in_vmem = pl.BlockSpec(memory_space=pltpu.VMEM)
    work = 2 * rows * keys * width
    held, sent = jnp.float32, jnp.bfloat16
    return pl.pallas_call(
        attention_kernel,
        out_shape=(
            jax.ShapeDtypeStruct((rows, width), jnp.bfloat16),
            jax.ShapeDtypeStruct((3, rows, double), held),
            jax.ShapeDtypeStruct((3 * rows + coarse_count, double), sent),
            jax.ShapeDtypeStruct((rows, double), sent),
            jax.ShapeDtypeStruct((2, rows, double), sent),
            jax.ShapeDtypeStruct((coarse_count, double), held),
        ),
        in_specs=[pl.BlockSpec(memory_space=pltpu.SMEM)] + [in_vmem] * (2 + len(blocks)),
        out_specs=(in_vmem,) * 6,
        scratch_shapes=[
            pltpu.VMEM((keys, 2 * rows), jnp.float32),
            pltpu.VMEM((keys, 2 * rows), jnp.float32),
        ],
        compiler_params=pltpu.CompilerParams(vmem_limit_bytes=40 * 2**20),
        cost_estimate=pl.CostEstimate(
            flops=5 * work, bytes_accessed=12 * 2**20, transcendentals=rows * keys * width // HEAD_DIM
        ),
    )(counts, query, upstream, *blocks)


def neighbour_counts(tile_counts):
    places = []
    for axis, size in zip(("row", "col"), tile_counts.shape):
        here = lax.axis_index(axis)
        odd = here % 2
        near = here + 1 - 2 * odd
        far = here - 1 + 2 * odd
        at = jnp.stack([here, near, far])
        places.append((at.clip(0, size - 1), (at >= 0) & (at < size)))
    (row_at, row_in), (col_at, col_in) = places
    found = tile_counts[row_at[None, :], col_at[:, None]]
    found = jnp.where(row_in[None, :] & col_in[:, None], found, 0).reshape(9)
    return jnp.concatenate([found, found[:1]]).astype(jnp.int32)


def per_device(
    fine_queries, fine_keys, fine_values, grad_out, coarse_keys, coarse_values, tile_counts
):
    rows, width = fine_queries.shape[2:]
    counts = neighbour_counts(tile_counts)
    low, high = jnp.bfloat16, jnp.float32
    own = jnp.concatenate([fine_keys[0, 0], fine_values[0, 0]], axis=-1)
    token = jnp.concatenate([coarse_keys, coarse_values], axis=-1)
    paired = exchange(own, "row", 1)
    token, paired = lax.optimization_barrier((token, paired))
    coarse = gather_first(token)
    skipped = skip_row(paired, 2)
    near_own, far_own = exchange(own, "col", 1), to_far(own, "col")
    coarse, skipped, far_own = lax.optimization_barrier((coarse, skipped, far_own))
    kept = gather_second(coarse)
    lines = jnp.stack([paired, skipped])
    near, far = exchange(lines, "col", 1), to_far(lines, "col")
    kept, far = lax.optimization_barrier((kept, far))
    other = exchange(kept, "col", 1)
    grad_q, own_terms, core_terms, far_own_terms, far_terms, kept_terms = attention(
        counts, fine_queries[0, 0], grad_out[0, 0], own, paired, skipped, near_own, near, far_own, far, kept, other
    )
    rows = own.shape[0]
    far_back = to_far(far_terms, "col")
    core_back = exchange(core_terms, "col", 1).astype(high)
    half = (kept_terms + core_back[3 * rows :]).astype(low)
    half, far_own_terms = lax.optimization_barrier((half, far_own_terms))
    line = own_terms + core_back[: 3 * rows].reshape(own_terms.shape)
    skipped_line = (line[2] + far_back[1].astype(high)).astype(low)
    skipped_line, far_own_terms = lax.optimization_barrier((skipped_line, far_own_terms))
    coarse_sum = scatter_coarse(half)
    forwarded = skip_row(skipped_line, -2).astype(high)
    paired_line = (line[1] + far_back[0].astype(high) + forwarded).astype(low)
    returned = exchange(paired_line, "row", 1).astype(high)
    total = (line[0] + to_far(far_own_terms, "col").astype(high) + returned).astype(low)
    return (
        grad_q[None, None],
        total[None, None, :, :width],
        total[None, None, :, width:],
        coarse_sum[:, :width],
        coarse_sum[:, width:],
    )


def solution(mesh):
    return jax.shard_map(
        per_device,
        mesh=mesh,
        in_specs=(
            P("row", "col", None, None),
            P("row", "col", None, None),
            P("row", "col", None, None),
            P("row", "col", None, None),
            P(("row", "col"), None),
            P(("row", "col"), None),
            P(),
        ),
        out_specs=(
            P("row", "col", None, None),
            P("row", "col", None, None),
            P("row", "col", None, None),
            P(("row", "col"), None),
            P(("row", "col"), None),
        ),
        check_vma=False,
    )
```

```python
import jax
import jax.numpy as jnp
from jax import lax
from jax.experimental import pallas as pl
from jax.experimental.pallas import tpu as pltpu
from jax.sharding import PartitionSpec as P

HEAD_DIM = 64
LANES = 128
SCALE = HEAD_DIM ** (-0.5)
NEGATIVE = -1e30

def exchange(block, axis, bit):
    return lax.ppermute(block, axis, [(i, i ^ bit) for i in range(lax.axis_size(axis))])


def to_far(block, axis):
    size = lax.axis_size(axis)
    return lax.ppermute(block, axis, [(i, (i + (1 if i % 2 else -1)) % size) for i in range(size)])


def skip_row(block, way):
    size = lax.axis_size("row")
    return lax.ppermute(block, "row", [(i, (i + (-way if i % 2 else way)) % size) for i in range(size)])


def place_groups():
    lines, columns = lax.axis_size("row"), lax.axis_size("col")
    half = columns // 2
    first = [
        [(z + y_hi) * columns + x_hi + x_lo + y_lo + core for x_hi in (0, half) for y_hi in range(2) for y_lo in range(0, 8, 2)]
        for z in range(0, lines, 2)
        for x_lo in range(0, half, 8)
        for core in range(2)
    ]
    second = [
        [(z + y_hi) * columns + x_hi + x_lo + y_lo + core for x_lo in range(0, half, 8) for z in range(0, lines, 2)]
        for x_hi in (0, half)
        for y_hi in range(2)
        for y_lo in range(0, 8, 2)
        for core in range(2)
    ]
    return first, second


def deal(block, groups):
    return lax.all_to_all(block, ("row", "col"), 0, 0, axis_index_groups=groups, tiled=True)


def gather_first(own):
    width = own.shape[-1]
    groups, _ = place_groups()
    members = len(groups[0])
    block = jnp.broadcast_to(own.reshape(1, 8, width // 8), (members, 8, width // 8))
    return deal(block, groups).reshape(members, width)


def gather_second(block):
    held, width = block.shape
    _, groups = place_groups()
    members = len(groups[0])
    return deal(jnp.broadcast_to(block, (members, held, width)), groups).reshape(members * held, width)


def scatter_second(block):
    width = block.shape[-1]
    first, second = place_groups()
    return deal(block.reshape(len(second[0]), len(first[0]), width), second).astype(jnp.float32).sum(axis=0)


def scatter_first(block):
    held, width = block.shape
    first, _ = place_groups()
    return deal(block.reshape(held, 8, width // 8), first).sum(axis=0).reshape(1, width)


def attention_kernel(
    counts, q_ref, g_ref, own_ref, pair_ref, skip_ref, near_own_ref, near_ref, far_own_ref, far_ref, kept_ref, other_ref,
    dq_ref, own_out, core_out, far_own_out, far_out, kept_out, p_ref, dp_ref,
):
    rows, width = q_ref.shape
    coarse_count = kept_ref.shape[0]
    step = min(rows, coarse_count)
    fine_in = (own_ref, pair_ref, skip_ref, near_own_ref, near_ref.at[0], near_ref.at[1], far_own_ref, far_ref.at[0], far_ref.at[1])
    fine_out = [own_out.at[at] for at in range(3)]
    fine_out += [core_out.at[at * rows : (at + 1) * rows] for at in range(3)]
    fine_out += [far_own_out, far_out.at[0], far_out.at[1]]
    tiles = [(fine_in[at], fine_out[at], rows, counts[at]) for at in range(9)]
    for ref, out, ahead in ((kept_ref, kept_out, 0), (other_ref, core_out, 3 * rows)):
        for start in range(0, coarse_count, step):
            tiles.append((ref.at[start : start + step], out.at[ahead + start : ahead + start + step], step, None))
    starts = []
    total = 0
    for tile in tiles:
        starts.append(total)
        total += tile[2]
    contract_last = (((1,), (1,)), ((), ()))
    contract_first = (((0,), (0,)), ((), ()))
    f32 = jnp.float32

    def stacked(block):
        first = lax.broadcasted_iota(jnp.int32, block.shape, 1) < HEAD_DIM
        zero = jnp.zeros_like(block)
        return jnp.concatenate([jnp.where(first, block, zero), jnp.where(first, zero, block)], axis=0)

    query_at = lax.broadcasted_iota(jnp.int32, (1, 2 * rows), 1)
    query_at = jnp.where(query_at >= rows, query_at - rows, query_at)
    query_live = (query_at < counts[9]).astype(f32)

    def pair(number, carry):
        lane = pl.multiple_of(number * LANES, LANES)
        at_k = pl.ds(lane, LANES)
        at_v = pl.ds(pl.multiple_of(width + number * LANES, LANES), LANES)
        query = stacked(q_ref[:, at_k] * jnp.asarray(SCALE, q_ref.dtype))
        upstream = stacked(g_ref[:, at_k])
        peak = jnp.full((1, 2 * rows), NEGATIVE, f32)
        for (ref, _, size, count), start in zip(tiles, starts):
            scores = lax.dot_general(ref[:, at_k], query, contract_last, preferred_element_type=f32)
            if count is not None:
                live = lax.broadcasted_iota(jnp.int32, scores.shape, 0) < count
                scores = jnp.where(live, scores, NEGATIVE)
            p_ref[start : start + size, :] = scores
            peak = jnp.maximum(peak, jnp.max(scores, axis=0, keepdims=True))
        norm = jnp.zeros((1, 2 * rows), f32)
        for (_, _, size, _), start in zip(tiles, starts):
            weights = jnp.exp(p_ref[start : start + size, :] - peak)
            p_ref[start : start + size, :] = weights
            norm = norm + jnp.sum(weights, axis=0, keepdims=True)
        inverse = query_live / norm
        delta = jnp.zeros((1, 2 * rows), f32)
        for (ref, out, size, _), start in zip(tiles, starts):
            probs = p_ref[start : start + size, :] * inverse
            probs_low = probs.astype(jnp.bfloat16)
            p_ref[start : start + size, :] = probs
            grad_probs = lax.dot_general(ref[:, at_v], upstream, contract_last, preferred_element_type=f32)
            dp_ref[start : start + size, :] = grad_probs
            delta = delta + jnp.sum(probs_low.astype(f32) * grad_probs, axis=0, keepdims=True)
            value_terms = jnp.dot(probs_low, upstream, preferred_element_type=f32)
            out[:, at_v] = value_terms.astype(out.dtype)
        grad_query = jnp.zeros((LANES, 2 * rows), f32)
        for (ref, out, size, _), start in zip(tiles, starts):
            span = slice(start, start + size)
            grad_low = (p_ref[span, :] * (dp_ref[span, :] - delta)).astype(jnp.bfloat16)
            key_terms = jnp.dot(grad_low, query, preferred_element_type=f32)
            out[:, at_k] = key_terms.astype(out.dtype)
            grad_query = grad_query + lax.dot_general(
                ref[:, at_k], grad_low, contract_first, preferred_element_type=f32
            )
        both = jnp.concatenate([grad_query[:HEAD_DIM, :rows], grad_query[HEAD_DIM:, rows:]], axis=0)
        dq_ref[:, at_k] = (both.T * SCALE).astype(dq_ref.dtype)
        return carry

    lax.fori_loop(0, width // LANES, pair, 0)


def attention(counts, query, upstream, *blocks):
    rows, width = query.shape
    double = 2 * width
    coarse_count = blocks[-1].shape[0]
    keys = 9 * rows + 2 * coarse_count
    in_vmem = pl.BlockSpec(memory_space=pltpu.VMEM)
    work = 2 * rows * keys * width
    held, sent = jnp.float32, jnp.bfloat16
    return pl.pallas_call(
        attention_kernel,
        out_shape=(
            jax.ShapeDtypeStruct((rows, width), jnp.bfloat16),
            jax.ShapeDtypeStruct((3, rows, double), held),
            jax.ShapeDtypeStruct((3 * rows + coarse_count, double), sent),
            jax.ShapeDtypeStruct((rows, double), sent),
            jax.ShapeDtypeStruct((2, rows, double), sent),
            jax.ShapeDtypeStruct((coarse_count, double), held),
        ),
        in_specs=[pl.BlockSpec(memory_space=pltpu.SMEM)] + [in_vmem] * (2 + len(blocks)),
        out_specs=(in_vmem,) * 6,
        scratch_shapes=[
            pltpu.VMEM((keys, 2 * rows), jnp.float32),
            pltpu.VMEM((keys, 2 * rows), jnp.float32),
        ],
        compiler_params=pltpu.CompilerParams(vmem_limit_bytes=40 * 2**20),
        cost_estimate=pl.CostEstimate(
            flops=5 * work, bytes_accessed=12 * 2**20, transcendentals=rows * keys * width // HEAD_DIM
        ),
    )(counts, query, upstream, *blocks)


def neighbour_counts(tile_counts):
    places = []
    for axis, size in zip(("row", "col"), tile_counts.shape):
        here = lax.axis_index(axis)
        odd = here % 2
        near = here + 1 - 2 * odd
        far = here - 1 + 2 * odd
        at = jnp.stack([here, near, far])
        places.append((at.clip(0, size - 1), (at >= 0) & (at < size)))
    (row_at, row_in), (col_at, col_in) = places
    found = tile_counts[row_at[None, :], col_at[:, None]]
    found = jnp.where(row_in[None, :] & col_in[:, None], found, 0).reshape(9)
    return jnp.concatenate([found, found[:1]]).astype(jnp.int32)


def per_device(
    fine_queries, fine_keys, fine_values, grad_out, coarse_keys, coarse_values, tile_counts
):
    rows, width = fine_queries.shape[2:]
    counts = neighbour_counts(tile_counts)
    low, high = jnp.bfloat16, jnp.float32
    own = jnp.concatenate([fine_keys[0, 0], fine_values[0, 0]], axis=-1)
    token = jnp.concatenate([coarse_keys, coarse_values], axis=-1)
    paired = exchange(own, "row", 1)
    coarse = gather_first(token)
    coarse, paired, again = lax.optimization_barrier((coarse, paired, own))
    skipped = skip_row(paired, 2)
    near_own, far_own = exchange(again, "col", 1), to_far(again, "col")
    kept = gather_second(coarse)
    skipped, far_own = lax.optimization_barrier((skipped, far_own))
    lines = jnp.stack([paired, skipped])
    near, far = exchange(lines, "col", 1), to_far(lines, "col")
    kept, far = lax.optimization_barrier((kept, far))
    other = exchange(kept, "col", 1)
    grad_q, own_terms, core_terms, far_own_terms, far_terms, kept_terms = attention(
        counts, fine_queries[0, 0], grad_out[0, 0], own, paired, skipped, near_own, near, far_own, far, kept, other
    )
    rows = own.shape[0]
    far_back = to_far(far_terms, "col")
    core_back = exchange(core_terms, "col", 1).astype(high)
    half = (kept_terms + core_back[3 * rows :]).astype(low)
    line = own_terms + core_back[: 3 * rows].reshape(own_terms.shape)
    skipped_line = (line[2] + far_back[1].astype(high)).astype(low)
    coarse_sum = scatter_second(half)
    coarse_sum, skipped_line, far_own_terms = lax.optimization_barrier((coarse_sum, skipped_line, far_own_terms))
    coarse_sum = scatter_first(coarse_sum)
    forwarded = skip_row(skipped_line, -2).astype(high)
    paired_line = (line[1] + far_back[0].astype(high) + forwarded).astype(low)
    returned = exchange(paired_line, "row", 1).astype(high)
    total = (line[0] + to_far(far_own_terms, "col").astype(high) + returned).astype(low)
    return (
        grad_q[None, None],
        total[None, None, :, :width],
        total[None, None, :, width:],
        coarse_sum[:, :width],
        coarse_sum[:, width:],
    )


def solution(mesh):
    return jax.shard_map(
        per_device,
        mesh=mesh,
        in_specs=(
            P("row", "col", None, None),
            P("row", "col", None, None),
            P("row", "col", None, None),
            P("row", "col", None, None),
            P(("row", "col"), None),
            P(("row", "col"), None),
            P(),
        ),
        out_specs=(
            P("row", "col", None, None),
            P("row", "col", None, None),
            P("row", "col", None, None),
            P(("row", "col"), None),
            P(("row", "col"), None),
        ),
        check_vma=False,
    )
```

```python
import jax
import jax.numpy as jnp
from jax import lax
from jax.experimental import pallas as pl
from jax.experimental.pallas import tpu as pltpu
from jax.sharding import PartitionSpec as P

HEAD_DIM = 64
LANES = 128
SCALE = HEAD_DIM ** (-0.5)
NEGATIVE = -1e30

def exchange(block, axis, bit):
    return lax.ppermute(block, axis, [(i, i ^ bit) for i in range(lax.axis_size(axis))])


def to_far(block, axis):
    size = lax.axis_size(axis)
    return lax.ppermute(block, axis, [(i, (i + (1 if i % 2 else -1)) % size) for i in range(size)])


def skip_row(block, way):
    size = lax.axis_size("row")
    return lax.ppermute(block, "row", [(i, (i + (-way if i % 2 else way)) % size) for i in range(size)])


def place_groups():
    lines, columns = lax.axis_size("row"), lax.axis_size("col")
    half = columns // 2
    first = [
        [(z + y_hi) * columns + x_hi + x_lo + y_lo + core for x_hi in (0, half) for y_hi in range(2) for y_lo in range(0, 8, 2)]
        for z in range(0, lines, 2)
        for x_lo in range(0, half, 8)
        for core in range(2)
    ]
    second = [
        [(z + y_hi) * columns + x_hi + x_lo + y_lo + core for x_lo in range(0, half, 8) for z in range(0, lines, 2)]
        for x_hi in (0, half)
        for y_hi in range(2)
        for y_lo in range(0, 8, 2)
        for core in range(2)
    ]
    return first, second


def deal(block, groups):
    return lax.all_to_all(block, ("row", "col"), 0, 0, axis_index_groups=groups, tiled=True)


def gather_first(own):
    width = own.shape[-1]
    groups, _ = place_groups()
    members = len(groups[0])
    block = jnp.broadcast_to(own.reshape(1, 8, width // 8), (members, 8, width // 8))
    return deal(block, groups).reshape(members, width)


def gather_second(block):
    held, width = block.shape
    _, groups = place_groups()
    members = len(groups[0])
    return deal(jnp.broadcast_to(block, (members, held, width)), groups).reshape(members * held, width)


def scatter_second(block):
    width = block.shape[-1]
    first, second = place_groups()
    return deal(block.reshape(len(second[0]), len(first[0]), width), second).astype(jnp.float32).sum(axis=0)


def scatter_first(block):
    held, width = block.shape
    first, _ = place_groups()
    return deal(block.reshape(held, 8, width // 8), first).sum(axis=0).reshape(1, width)


def attention_kernel(
    counts, q_ref, g_ref, own_ref, pair_ref, skip_ref, near_own_ref, near_ref, far_own_ref, far_ref, kept_ref, other_ref,
    dq_ref, own_out, core_out, far_own_out, far_out, kept_out, p_ref, dp_ref,
):
    rows, width = q_ref.shape
    coarse_count = kept_ref.shape[0]
    step = min(rows, coarse_count)
    fine_in = (own_ref, pair_ref, skip_ref, near_own_ref, near_ref.at[0], near_ref.at[1], far_own_ref, far_ref.at[0], far_ref.at[1])
    fine_out = [own_out.at[at] for at in range(3)]
    fine_out += [core_out.at[at * rows : (at + 1) * rows] for at in range(3)]
    fine_out += [far_own_out, far_out.at[0], far_out.at[1]]
    tiles = [(fine_in[at], fine_out[at], rows, counts[at]) for at in range(9)]
    for ref, out, ahead in ((kept_ref, kept_out, 0), (other_ref, core_out, 3 * rows)):
        for start in range(0, coarse_count, step):
            tiles.append((ref.at[start : start + step], out.at[ahead + start : ahead + start + step], step, None))
    starts = []
    total = 0
    for tile in tiles:
        starts.append(total)
        total += tile[2]
    contract_last = (((1,), (1,)), ((), ()))
    contract_first = (((0,), (0,)), ((), ()))
    f32 = jnp.float32

    def stacked(block):
        first = lax.broadcasted_iota(jnp.int32, block.shape, 1) < HEAD_DIM
        zero = jnp.zeros_like(block)
        return jnp.concatenate([jnp.where(first, block, zero), jnp.where(first, zero, block)], axis=0)

    query_at = lax.broadcasted_iota(jnp.int32, (1, 2 * rows), 1)
    query_at = jnp.where(query_at >= rows, query_at - rows, query_at)
    query_live = (query_at < counts[9]).astype(f32)

    def pair(number, carry):
        lane = pl.multiple_of(number * LANES, LANES)
        at_k = pl.ds(lane, LANES)
        at_v = pl.ds(pl.multiple_of(width + number * LANES, LANES), LANES)
        query = stacked(q_ref[:, at_k] * jnp.asarray(SCALE, q_ref.dtype))
        upstream = stacked(g_ref[:, at_k])
        peak = jnp.full((1, 2 * rows), NEGATIVE, f32)
        for (ref, _, size, count), start in zip(tiles, starts):
            scores = lax.dot_general(ref[:, at_k], query, contract_last, preferred_element_type=f32)
            if count is not None:
                live = lax.broadcasted_iota(jnp.int32, scores.shape, 0) < count
                scores = jnp.where(live, scores, NEGATIVE)
            p_ref[start : start + size, :] = scores
            peak = jnp.maximum(peak, jnp.max(scores, axis=0, keepdims=True))
        norm = jnp.zeros((1, 2 * rows), f32)
        for (_, _, size, _), start in zip(tiles, starts):
            weights = jnp.exp(p_ref[start : start + size, :] - peak)
            p_ref[start : start + size, :] = weights
            norm = norm + jnp.sum(weights, axis=0, keepdims=True)
        inverse = query_live / norm
        delta = jnp.zeros((1, 2 * rows), f32)
        for (ref, out, size, _), start in zip(tiles, starts):
            probs = p_ref[start : start + size, :] * inverse
            probs_low = probs.astype(jnp.bfloat16)
            p_ref[start : start + size, :] = probs
            grad_probs = lax.dot_general(ref[:, at_v], upstream, contract_last, preferred_element_type=f32)
            dp_ref[start : start + size, :] = grad_probs
            delta = delta + jnp.sum(probs_low.astype(f32) * grad_probs, axis=0, keepdims=True)
            value_terms = jnp.dot(probs_low, upstream, preferred_element_type=f32)
            out[:, at_v] = value_terms.astype(out.dtype)
        grad_query = jnp.zeros((LANES, 2 * rows), f32)
        for (ref, out, size, _), start in zip(tiles, starts):
            span = slice(start, start + size)
            grad_low = (p_ref[span, :] * (dp_ref[span, :] - delta)).astype(jnp.bfloat16)
            key_terms = jnp.dot(grad_low, query, preferred_element_type=f32)
            out[:, at_k] = key_terms.astype(out.dtype)
            grad_query = grad_query + lax.dot_general(
                ref[:, at_k], grad_low, contract_first, preferred_element_type=f32
            )
        both = jnp.concatenate([grad_query[:HEAD_DIM, :rows], grad_query[HEAD_DIM:, rows:]], axis=0)
        dq_ref[:, at_k] = (both.T * SCALE).astype(dq_ref.dtype)
        return carry

    lax.fori_loop(0, width // LANES, pair, 0)


def attention(counts, query, upstream, *blocks):
    rows, width = query.shape
    double = 2 * width
    coarse_count = blocks[-1].shape[0]
    keys = 9 * rows + 2 * coarse_count
    in_vmem = pl.BlockSpec(memory_space=pltpu.VMEM)
    work = 2 * rows * keys * width
    held, sent = jnp.float32, jnp.bfloat16
    return pl.pallas_call(
        attention_kernel,
        out_shape=(
            jax.ShapeDtypeStruct((rows, width), jnp.bfloat16),
            jax.ShapeDtypeStruct((3, rows, double), held),
            jax.ShapeDtypeStruct((3 * rows + coarse_count, double), sent),
            jax.ShapeDtypeStruct((rows, double), sent),
            jax.ShapeDtypeStruct((2, rows, double), sent),
            jax.ShapeDtypeStruct((coarse_count, double), held),
        ),
        in_specs=[pl.BlockSpec(memory_space=pltpu.SMEM)] + [in_vmem] * (2 + len(blocks)),
        out_specs=(in_vmem,) * 6,
        scratch_shapes=[
            pltpu.VMEM((keys, 2 * rows), jnp.float32),
            pltpu.VMEM((keys, 2 * rows), jnp.float32),
        ],
        compiler_params=pltpu.CompilerParams(vmem_limit_bytes=50 * 2**20),
        cost_estimate=pl.CostEstimate(
            flops=5 * work, bytes_accessed=12 * 2**20, transcendentals=rows * keys * width // HEAD_DIM
        ),
    )(counts, query, upstream, *blocks)


def neighbour_counts(tile_counts):
    places = []
    for axis, size in zip(("row", "col"), tile_counts.shape):
        here = lax.axis_index(axis)
        odd = here % 2
        near = here + 1 - 2 * odd
        far = here - 1 + 2 * odd
        at = jnp.stack([here, near, far])
        places.append((at.clip(0, size - 1), (at >= 0) & (at < size)))
    (row_at, row_in), (col_at, col_in) = places
    found = tile_counts[row_at[None, :], col_at[:, None]]
    found = jnp.where(row_in[None, :] & col_in[:, None], found, 0).reshape(9)
    return jnp.concatenate([found, found[:1]]).astype(jnp.int32)


def per_device(
    fine_queries, fine_keys, fine_values, grad_out, coarse_keys, coarse_values, tile_counts
):
    rows, width = fine_queries.shape[2:]
    counts = neighbour_counts(tile_counts)
    low, high = jnp.bfloat16, jnp.float32
    own = jnp.concatenate([fine_keys[0, 0], fine_values[0, 0]], axis=-1)
    token = jnp.concatenate([coarse_keys, coarse_values], axis=-1)
    paired = exchange(own, "row", 1)
    coarse = gather_first(token)
    coarse, paired, again = lax.optimization_barrier((coarse, paired, own))
    skipped = skip_row(paired, 2)
    near_own, far_own = exchange(again, "col", 1), to_far(again, "col")
    coarse, skipped, far_own = lax.optimization_barrier((coarse, skipped, far_own))
    kept = gather_second(coarse)
    lines = jnp.stack([paired, skipped])
    near, far = exchange(lines, "col", 1), to_far(lines, "col")
    kept, far = lax.optimization_barrier((kept, far))
    other = exchange(kept, "col", 1)
    grad_q, own_terms, core_terms, far_own_terms, far_terms, kept_terms = attention(
        counts, fine_queries[0, 0], grad_out[0, 0], own, paired, skipped, near_own, near, far_own, far, kept, other
    )
    rows = own.shape[0]
    far_back = to_far(far_terms, "col")
    core_back = exchange(core_terms, "col", 1).astype(high)
    half = (kept_terms + core_back[3 * rows :]).astype(low)
    line = own_terms + core_back[: 3 * rows].reshape(own_terms.shape)
    skipped_line = (line[2] + far_back[1].astype(high)).astype(low)
    coarse_sum = scatter_second(half)
    skipped_line, far_own_terms = lax.optimization_barrier((skipped_line, far_own_terms))
    forwarded = skip_row(skipped_line, -2).astype(high)
    coarse_sum, forwarded = lax.optimization_barrier((coarse_sum, forwarded))
    coarse_sum = scatter_first(coarse_sum)
    paired_line = (line[1] + far_back[0].astype(high) + forwarded).astype(low)
    returned = exchange(paired_line, "row", 1).astype(high)
    total = (line[0] + to_far(far_own_terms, "col").astype(high) + returned).astype(low)
    return (
        grad_q[None, None],
        total[None, None, :, :width],
        total[None, None, :, width:],
        coarse_sum[:, :width],
        coarse_sum[:, width:],
    )


def solution(mesh):
    return jax.shard_map(
        per_device,
        mesh=mesh,
        in_specs=(
            P("row", "col", None, None),
            P("row", "col", None, None),
            P("row", "col", None, None),
            P("row", "col", None, None),
            P(("row", "col"), None),
            P(("row", "col"), None),
            P(),
        ),
        out_specs=(
            P("row", "col", None, None),
            P("row", "col", None, None),
            P("row", "col", None, None),
            P(("row", "col"), None),
            P(("row", "col"), None),
        ),
        check_vma=False,
    )
```

```python
import jax
import jax.numpy as jnp
from jax import lax
from jax.experimental import pallas as pl
from jax.experimental.pallas import tpu as pltpu
from jax.sharding import PartitionSpec as P

HEAD_DIM = 64
LANES = 128
SCALE = HEAD_DIM ** (-0.5)
NEGATIVE = -1e30

def exchange(block, axis, bit):
    return lax.ppermute(block, axis, [(i, i ^ bit) for i in range(lax.axis_size(axis))])


def to_far(block, axis):
    size = lax.axis_size(axis)
    return lax.ppermute(block, axis, [(i, (i + (1 if i % 2 else -1)) % size) for i in range(size)])


def skip_row(block, way):
    size = lax.axis_size("row")
    return lax.ppermute(block, "row", [(i, (i + (-way if i % 2 else way)) % size) for i in range(size)])


def place_groups():
    lines, columns = lax.axis_size("row"), lax.axis_size("col")
    half = columns // 2
    first = [
        [(z + y_hi) * columns + x_hi + x_lo + y_lo + core for x_hi in (0, half) for y_hi in range(2) for y_lo in range(0, 8, 2)]
        for z in range(0, lines, 2)
        for x_lo in range(0, half, 8)
        for core in range(2)
    ]
    second = [
        [(z + y_hi) * columns + x_hi + x_lo + y_lo + core for x_lo in range(0, half, 8) for z in range(0, lines, 2)]
        for x_hi in (0, half)
        for y_hi in range(2)
        for y_lo in range(0, 8, 2)
        for core in range(2)
    ]
    return first, second


def deal(block, groups):
    return lax.all_to_all(block, ("row", "col"), 0, 0, axis_index_groups=groups, tiled=True)


def gather_first(own):
    width = own.shape[-1]
    groups, _ = place_groups()
    members = len(groups[0])
    block = jnp.broadcast_to(own.reshape(1, 8, width // 8), (members, 8, width // 8))
    return deal(block, groups).reshape(members, width)


def gather_second(block):
    held, width = block.shape
    _, groups = place_groups()
    members = len(groups[0])
    return deal(jnp.broadcast_to(block, (members, held, width)), groups).reshape(members * held, width)


def scatter_second(block):
    width = block.shape[-1]
    first, second = place_groups()
    return deal(block.reshape(len(second[0]), len(first[0]), width), second).astype(jnp.float32).sum(axis=0)


def scatter_first(block):
    held, width = block.shape
    first, _ = place_groups()
    return deal(block.reshape(held, 8, width // 8), first).sum(axis=0).reshape(1, width)


def attention_kernel(
    counts, q_ref, g_ref, own_ref, near_ref, far_ref, kept_ref, other_ref,
    dq_ref, own_out, core_out, far_out, kept_out, p_ref, dp_ref,
):
    rows, width = q_ref.shape
    coarse_count = kept_ref.shape[0]
    step = min(rows, coarse_count)
    fine_in = [ref.at[at] for ref in (own_ref, near_ref, far_ref) for at in range(3)]
    fine_out = [own_out.at[at] for at in range(3)]
    fine_out += [core_out.at[at * rows : (at + 1) * rows] for at in range(3)]
    fine_out += [far_out.at[at] for at in range(3)]
    tiles = [(fine_in[at], fine_out[at], rows, counts[at]) for at in range(9)]
    for ref, out, ahead in ((kept_ref, kept_out, 0), (other_ref, core_out, 3 * rows)):
        for start in range(0, coarse_count, step):
            tiles.append((ref.at[start : start + step], out.at[ahead + start : ahead + start + step], step, None))
    starts = []
    total = 0
    for tile in tiles:
        starts.append(total)
        total += tile[2]
    contract_last = (((1,), (1,)), ((), ()))
    contract_first = (((0,), (0,)), ((), ()))
    f32 = jnp.float32

    def stacked(block):
        first = lax.broadcasted_iota(jnp.int32, block.shape, 1) < HEAD_DIM
        zero = jnp.zeros_like(block)
        return jnp.concatenate([jnp.where(first, block, zero), jnp.where(first, zero, block)], axis=0)

    query_at = lax.broadcasted_iota(jnp.int32, (1, 2 * rows), 1)
    query_at = jnp.where(query_at >= rows, query_at - rows, query_at)
    query_live = (query_at < counts[9]).astype(f32)

    def pair(number, carry):
        lane = pl.multiple_of(number * LANES, LANES)
        at_k = pl.ds(lane, LANES)
        at_v = pl.ds(pl.multiple_of(width + number * LANES, LANES), LANES)
        query = stacked(q_ref[:, at_k] * jnp.asarray(SCALE, q_ref.dtype))
        upstream = stacked(g_ref[:, at_k])
        peak = jnp.full((1, 2 * rows), NEGATIVE, f32)
        for (ref, _, size, count), start in zip(tiles, starts):
            scores = lax.dot_general(ref[:, at_k], query, contract_last, preferred_element_type=f32)
            if count is not None:
                live = lax.broadcasted_iota(jnp.int32, scores.shape, 0) < count
                scores = jnp.where(live, scores, NEGATIVE)
            p_ref[start : start + size, :] = scores
            peak = jnp.maximum(peak, jnp.max(scores, axis=0, keepdims=True))
        norm = jnp.zeros((1, 2 * rows), f32)
        for (_, _, size, _), start in zip(tiles, starts):
            weights = jnp.exp(p_ref[start : start + size, :] - peak)
            p_ref[start : start + size, :] = weights
            norm = norm + jnp.sum(weights, axis=0, keepdims=True)
        inverse = query_live / norm
        delta = jnp.zeros((1, 2 * rows), f32)
        for (ref, out, size, _), start in zip(tiles, starts):
            probs = p_ref[start : start + size, :] * inverse
            probs_low = probs.astype(jnp.bfloat16)
            p_ref[start : start + size, :] = probs
            grad_probs = lax.dot_general(ref[:, at_v], upstream, contract_last, preferred_element_type=f32)
            dp_ref[start : start + size, :] = grad_probs
            delta = delta + jnp.sum(probs_low.astype(f32) * grad_probs, axis=0, keepdims=True)
            value_terms = jnp.dot(probs_low, upstream, preferred_element_type=f32)
            out[:, at_v] = value_terms.astype(out.dtype)
        grad_query = jnp.zeros((LANES, 2 * rows), f32)
        for (ref, out, size, _), start in zip(tiles, starts):
            span = slice(start, start + size)
            grad_low = (p_ref[span, :] * (dp_ref[span, :] - delta)).astype(jnp.bfloat16)
            key_terms = jnp.dot(grad_low, query, preferred_element_type=f32)
            out[:, at_k] = key_terms.astype(out.dtype)
            grad_query = grad_query + lax.dot_general(
                ref[:, at_k], grad_low, contract_first, preferred_element_type=f32
            )
        both = jnp.concatenate([grad_query[:HEAD_DIM, :rows], grad_query[HEAD_DIM:, rows:]], axis=0)
        dq_ref[:, at_k] = (both.T * SCALE).astype(dq_ref.dtype)
        return carry

    lax.fori_loop(0, width // LANES, pair, 0)


def attention(counts, query, upstream, *blocks):
    rows, width = query.shape
    double = 2 * width
    coarse_count = blocks[-1].shape[0]
    keys = 9 * rows + 2 * coarse_count
    in_vmem = pl.BlockSpec(memory_space=pltpu.VMEM)
    work = 2 * rows * keys * width
    held, sent = jnp.float32, jnp.bfloat16
    return pl.pallas_call(
        attention_kernel,
        out_shape=(
            jax.ShapeDtypeStruct((rows, width), jnp.bfloat16),
            jax.ShapeDtypeStruct((3, rows, double), held),
            jax.ShapeDtypeStruct((3 * rows + coarse_count, double), sent),
            jax.ShapeDtypeStruct((3, rows, double), sent),
            jax.ShapeDtypeStruct((coarse_count, double), held),
        ),
        in_specs=[pl.BlockSpec(memory_space=pltpu.SMEM)] + [in_vmem] * (2 + len(blocks)),
        out_specs=(in_vmem,) * 5,
        scratch_shapes=[
            pltpu.VMEM((keys, 2 * rows), jnp.float32),
            pltpu.VMEM((keys, 2 * rows), jnp.float32),
        ],
        compiler_params=pltpu.CompilerParams(vmem_limit_bytes=48 * 2**20),
        cost_estimate=pl.CostEstimate(
            flops=5 * work, bytes_accessed=12 * 2**20, transcendentals=rows * keys * width // HEAD_DIM
        ),
    )(counts, query, upstream, *blocks)


def neighbour_counts(tile_counts):
    places = []
    for axis, size in zip(("row", "col"), tile_counts.shape):
        here = lax.axis_index(axis)
        odd = here % 2
        near = here + 1 - 2 * odd
        far = here - 1 + 2 * odd
        at = jnp.stack([here, near, far])
        places.append((at.clip(0, size - 1), (at >= 0) & (at < size)))
    (row_at, row_in), (col_at, col_in) = places
    found = tile_counts[row_at[None, :], col_at[:, None]]
    found = jnp.where(row_in[None, :] & col_in[:, None], found, 0).reshape(9)
    return jnp.concatenate([found, found[:1]]).astype(jnp.int32)


def per_device(
    fine_queries, fine_keys, fine_values, grad_out, coarse_keys, coarse_values, tile_counts
):
    rows, width = fine_queries.shape[2:]
    counts = neighbour_counts(tile_counts)
    low, high = jnp.bfloat16, jnp.float32
    own = jnp.concatenate([fine_keys[0, 0], fine_values[0, 0]], axis=-1)
    token = jnp.concatenate([coarse_keys, coarse_values], axis=-1)
    paired = exchange(own, "row", 1)
    coarse = gather_first(token)
    coarse, paired = lax.optimization_barrier((coarse, paired))
    column = jnp.stack([own, paired, skip_row(paired, 2)])
    near, far = exchange(column, "col", 1), to_far(column, "col")
    coarse, near = lax.optimization_barrier((coarse, near))
    kept = gather_second(coarse)
    other = exchange(kept, "col", 1)
    grad_q, own_terms, core_terms, far_terms, kept_terms = attention(
        counts, fine_queries[0, 0], grad_out[0, 0], column, near, far, kept, other
    )
    rows = own.shape[0]
    far_back = to_far(far_terms, "col")
    core_back = exchange(core_terms, "col", 1).astype(high)
    half = (kept_terms + core_back[3 * rows :]).astype(low)
    line = own_terms + core_back[: 3 * rows].reshape(own_terms.shape)
    coarse_sum = scatter_second(half)
    line = line + far_back.astype(high)
    coarse_sum, line = lax.optimization_barrier((coarse_sum, line))
    forwarded = skip_row(line[2].astype(low), -2).astype(high)
    coarse_sum = scatter_first(coarse_sum)
    returned = exchange((line[1] + forwarded).astype(low), "row", 1).astype(high)
    total = (line[0] + returned).astype(low)
    return (
        grad_q[None, None],
        total[None, None, :, :width],
        total[None, None, :, width:],
        coarse_sum[:, :width],
        coarse_sum[:, width:],
    )


def solution(mesh):
    return jax.shard_map(
        per_device,
        mesh=mesh,
        in_specs=(
            P("row", "col", None, None),
            P("row", "col", None, None),
            P("row", "col", None, None),
            P("row", "col", None, None),
            P(("row", "col"), None),
            P(("row", "col"), None),
            P(),
        ),
        out_specs=(
            P("row", "col", None, None),
            P("row", "col", None, None),
            P("row", "col", None, None),
            P(("row", "col"), None),
            P(("row", "col"), None),
        ),
        check_vma=False,
    )
```

```python
import jax
import jax.numpy as jnp
from jax import lax
from jax.experimental import pallas as pl
from jax.experimental.pallas import tpu as pltpu
from jax.sharding import PartitionSpec as P

HEAD_DIM = 64
LANES = 128
SCALE = HEAD_DIM ** (-0.5)
NEGATIVE = -1e30

def exchange(block, axis, bit):
    return lax.ppermute(block, axis, [(i, i ^ bit) for i in range(lax.axis_size(axis))])


def to_far(block, axis):
    size = lax.axis_size(axis)
    return lax.ppermute(block, axis, [(i, (i + (1 if i % 2 else -1)) % size) for i in range(size)])


def skip_row(block, way):
    size = lax.axis_size("row")
    return lax.ppermute(block, "row", [(i, (i + (-way if i % 2 else way)) % size) for i in range(size)])


def place_groups():
    lines, columns = lax.axis_size("row"), lax.axis_size("col")
    half = columns // 2
    first = [
        [(z + y_hi) * columns + x_hi + x_lo + y_lo + core for x_hi in (0, half) for y_hi in range(2) for y_lo in range(0, 8, 2)]
        for z in range(0, lines, 2)
        for x_lo in range(0, half, 8)
        for core in range(2)
    ]
    second = [
        [(z + y_hi) * columns + x_hi + x_lo + y_lo + core for x_lo in range(0, half, 8) for z in range(0, lines, 2)]
        for x_hi in (0, half)
        for y_hi in range(2)
        for y_lo in range(0, 8, 2)
        for core in range(2)
    ]
    return first, second


def deal(block, groups):
    return lax.all_to_all(block, ("row", "col"), 0, 0, axis_index_groups=groups, tiled=True)


def gather_line(own):
    lines = lax.axis_size("row")
    tile = (8, own.shape[-1] // 8)
    return lax.all_to_all(jnp.broadcast_to(own.reshape(1, *tile), (lines, *tile)), "row", 0, 0, tiled=True)


def gather_rest(block):
    lines, *tile = block.shape
    columns = lax.axis_size("col")
    members = columns // 2
    same_core = [list(range(core, columns, 2)) for core in range(2)]
    block = jnp.broadcast_to(block[None], (members, lines, *tile))
    block = lax.all_to_all(block, "col", 0, 0, axis_index_groups=same_core, tiled=True)
    block = block.reshape(2, columns // 16, 4, lines // 2, 2, *tile).transpose(1, 3, 0, 4, 2, 5, 6)
    return block.reshape(members * lines, tile[0] * tile[1])


def scatter_second(block):
    width = block.shape[-1]
    first, second = place_groups()
    return deal(block.reshape(len(second[0]), len(first[0]), width), second).astype(jnp.float32).sum(axis=0)


def scatter_first(block):
    held, width = block.shape
    first, _ = place_groups()
    return deal(block.reshape(held, 8, width // 8), first).sum(axis=0).reshape(1, width)


def attention_kernel(
    counts, q_ref, g_ref, own_ref, near_ref, far_ref, kept_ref, other_ref,
    dq_ref, own_out, core_out, far_out, kept_out, p_ref, dp_ref,
):
    rows, width = q_ref.shape
    coarse_count = kept_ref.shape[0]
    step = min(rows, coarse_count)
    fine_in = [ref.at[at] for ref in (own_ref, near_ref, far_ref) for at in range(3)]
    fine_out = [own_out.at[at] for at in range(3)]
    fine_out += [core_out.at[at * rows : (at + 1) * rows] for at in range(3)]
    fine_out += [far_out.at[at] for at in range(3)]
    tiles = [(fine_in[at], fine_out[at], rows, counts[at]) for at in range(9)]
    for ref, out, ahead in ((kept_ref, kept_out, 0), (other_ref, core_out, 3 * rows)):
        for start in range(0, coarse_count, step):
            tiles.append((ref.at[start : start + step], out.at[ahead + start : ahead + start + step], step, None))
    starts = []
    total = 0
    for tile in tiles:
        starts.append(total)
        total += tile[2]
    contract_last = (((1,), (1,)), ((), ()))
    contract_first = (((0,), (0,)), ((), ()))
    f32 = jnp.float32

    def stacked(block):
        first = lax.broadcasted_iota(jnp.int32, block.shape, 1) < HEAD_DIM
        zero = jnp.zeros_like(block)
        return jnp.concatenate([jnp.where(first, block, zero), jnp.where(first, zero, block)], axis=0)

    query_at = lax.broadcasted_iota(jnp.int32, (1, 2 * rows), 1)
    query_at = jnp.where(query_at >= rows, query_at - rows, query_at)
    query_live = (query_at < counts[9]).astype(f32)

    def pair(number, carry):
        lane = pl.multiple_of(number * LANES, LANES)
        at_k = pl.ds(lane, LANES)
        at_v = pl.ds(pl.multiple_of(width + number * LANES, LANES), LANES)
        query = stacked(q_ref[:, at_k] * jnp.asarray(SCALE, q_ref.dtype))
        upstream = stacked(g_ref[:, at_k])
        peak = jnp.full((1, 2 * rows), NEGATIVE, f32)
        for (ref, _, size, count), start in zip(tiles, starts):
            scores = lax.dot_general(ref[:, at_k], query, contract_last, preferred_element_type=f32)
            if count is not None:
                live = lax.broadcasted_iota(jnp.int32, scores.shape, 0) < count
                scores = jnp.where(live, scores, NEGATIVE)
            p_ref[start : start + size, :] = scores
            peak = jnp.maximum(peak, jnp.max(scores, axis=0, keepdims=True))
        norm = jnp.zeros((1, 2 * rows), f32)
        for (_, _, size, _), start in zip(tiles, starts):
            weights = jnp.exp(p_ref[start : start + size, :] - peak)
            p_ref[start : start + size, :] = weights
            norm = norm + jnp.sum(weights, axis=0, keepdims=True)
        inverse = query_live / norm
        delta = jnp.zeros((1, 2 * rows), f32)
        for (ref, out, size, _), start in zip(tiles, starts):
            probs = p_ref[start : start + size, :] * inverse
            probs_low = probs.astype(jnp.bfloat16)
            p_ref[start : start + size, :] = probs
            grad_probs = lax.dot_general(ref[:, at_v], upstream, contract_last, preferred_element_type=f32)
            dp_ref[start : start + size, :] = grad_probs
            delta = delta + jnp.sum(probs_low.astype(f32) * grad_probs, axis=0, keepdims=True)
            value_terms = jnp.dot(probs_low, upstream, preferred_element_type=f32)
            out[:, at_v] = value_terms.astype(out.dtype)
        grad_query = jnp.zeros((LANES, 2 * rows), f32)
        for (ref, out, size, _), start in zip(tiles, starts):
            span = slice(start, start + size)
            grad_low = (p_ref[span, :] * (dp_ref[span, :] - delta)).astype(jnp.bfloat16)
            key_terms = jnp.dot(grad_low, query, preferred_element_type=f32)
            out[:, at_k] = key_terms.astype(out.dtype)
            grad_query = grad_query + lax.dot_general(
                ref[:, at_k], grad_low, contract_first, preferred_element_type=f32
            )
        both = jnp.concatenate([grad_query[:HEAD_DIM, :rows], grad_query[HEAD_DIM:, rows:]], axis=0)
        dq_ref[:, at_k] = (both.T * SCALE).astype(dq_ref.dtype)
        return carry

    lax.fori_loop(0, width // LANES, pair, 0)


def attention(counts, query, upstream, *blocks):
    rows, width = query.shape
    double = 2 * width
    coarse_count = blocks[-1].shape[0]
    keys = 9 * rows + 2 * coarse_count
    in_vmem = pl.BlockSpec(memory_space=pltpu.VMEM)
    work = 2 * rows * keys * width
    held, sent = jnp.float32, jnp.bfloat16
    return pl.pallas_call(
        attention_kernel,
        out_shape=(
            jax.ShapeDtypeStruct((rows, width), jnp.bfloat16),
            jax.ShapeDtypeStruct((3, rows, double), held),
            jax.ShapeDtypeStruct((3 * rows + coarse_count, double), sent),
            jax.ShapeDtypeStruct((3, rows, double), sent),
            jax.ShapeDtypeStruct((coarse_count, double), held),
        ),
        in_specs=[pl.BlockSpec(memory_space=pltpu.SMEM)] + [in_vmem] * (2 + len(blocks)),
        out_specs=(in_vmem,) * 5,
        scratch_shapes=[
            pltpu.VMEM((keys, 2 * rows), jnp.float32),
            pltpu.VMEM((keys, 2 * rows), jnp.float32),
        ],
        compiler_params=pltpu.CompilerParams(vmem_limit_bytes=48 * 2**20),
        cost_estimate=pl.CostEstimate(
            flops=5 * work, bytes_accessed=12 * 2**20, transcendentals=rows * keys * width // HEAD_DIM
        ),
    )(counts, query, upstream, *blocks)


def neighbour_counts(tile_counts):
    places = []
    for axis, size in zip(("row", "col"), tile_counts.shape):
        here = lax.axis_index(axis)
        odd = here % 2
        near = here + 1 - 2 * odd
        far = here - 1 + 2 * odd
        at = jnp.stack([here, near, far])
        places.append((at.clip(0, size - 1), (at >= 0) & (at < size)))
    (row_at, row_in), (col_at, col_in) = places
    found = tile_counts[row_at[None, :], col_at[:, None]]
    found = jnp.where(row_in[None, :] & col_in[:, None], found, 0).reshape(9)
    return jnp.concatenate([found, found[:1]]).astype(jnp.int32)


def per_device(
    fine_queries, fine_keys, fine_values, grad_out, coarse_keys, coarse_values, tile_counts
):
    rows, width = fine_queries.shape[2:]
    counts = neighbour_counts(tile_counts)
    low, high = jnp.bfloat16, jnp.float32
    own = jnp.concatenate([fine_keys[0, 0], fine_values[0, 0]], axis=-1)
    token = jnp.concatenate([coarse_keys, coarse_values], axis=-1)
    paired = exchange(own, "row", 1)
    coarse = gather_line(token)
    coarse, paired = lax.optimization_barrier((coarse, paired))
    kept = gather_rest(coarse)
    column = jnp.stack([own, paired, skip_row(paired, 2)])
    near, far = exchange(column, "col", 1), to_far(column, "col")
    other = exchange(kept, "col", 1)
    grad_q, own_terms, core_terms, far_terms, kept_terms = attention(
        counts, fine_queries[0, 0], grad_out[0, 0], column, near, far, kept, other
    )
    rows = own.shape[0]
    far_back = to_far(far_terms, "col")
    core_back = exchange(core_terms, "col", 1).astype(high)
    half = (kept_terms + core_back[3 * rows :]).astype(low)
    line = own_terms + core_back[: 3 * rows].reshape(own_terms.shape)
    coarse_sum = scatter_second(half)
    line = line + far_back.astype(high)
    coarse_sum, line = lax.optimization_barrier((coarse_sum, line))
    forwarded = skip_row(line[2].astype(low), -2).astype(high)
    coarse_sum = scatter_first(coarse_sum)
    returned = exchange((line[1] + forwarded).astype(low), "row", 1).astype(high)
    total = (line[0] + returned).astype(low)
    return (
        grad_q[None, None],
        total[None, None, :, :width],
        total[None, None, :, width:],
        coarse_sum[:, :width],
        coarse_sum[:, width:],
    )


def solution(mesh):
    return jax.shard_map(
        per_device,
        mesh=mesh,
        in_specs=(
            P("row", "col", None, None),
            P("row", "col", None, None),
            P("row", "col", None, None),
            P("row", "col", None, None),
            P(("row", "col"), None),
            P(("row", "col"), None),
            P(),
        ),
        out_specs=(
            P("row", "col", None, None),
            P("row", "col", None, None),
            P("row", "col", None, None),
            P(("row", "col"), None),
            P(("row", "col"), None),
        ),
        check_vma=False,
    )
```
